32 devices in a mesh: groups: 2 (over y), blk: 16 (over z, x, core).
Axes of the slice: x: 2, y: 2, z: 4, core: 2. Of those that a mesh axis runs over, the one named last changes fastest.
Arguments:
- crack_energy: float32 [32768], P(('groups', 'blk')), parts along dimension 0, may hold values from 0.05 to 4
- weights: float32 [8, 32768], P(None, ('groups', 'blk')), parts along dimension 1, may hold values from 0 to 0.25
- elastic_stress: float32 [6, 32768], P(None, ('groups', 'blk')), parts along dimension 1, may hold values from -6 to 6
- owner_rank: int32 [32768, 1], P(('groups', 'blk')), parts along dimension 0, may hold values from 0 to 15; in each aligned block of 1024 rows (0 to 1023, 1024 to 2047, ...) at most 128 rows name the same one
- local_block: int32 [32768], P(('groups', 'blk')), parts along dimension 0, may hold values from 0 to 255
- base_cell: int32 [32768], P(('groups', 'blk')), parts along dimension 0, may hold values from 0 to 26
- prior_damage: float32 [256, 16, 128], P(('groups', 'blk')), parts along dimension 0, may hold values from 0 to 0.6
- toughness: float32 [256, 16, 128], P(('groups', 'blk')), parts along dimension 0, may hold values from 0.5 to 2
- active_block: int32 [8192], P(('groups', 'blk')), parts along dimension 0, may hold values 0 or 1
Outputs:
- damage: float32 [256, 16, 128], P(('groups', 'blk')), parts along dimension 0
- degraded_stress: float32 [6, 32768], P(None, ('groups', 'blk')), parts along dimension 1
The draws below stay inside these ranges and needn't reach their ends.
There are 2 independent parts, one for each index of `groups`. The reference program is written for one: setup_inputs(seed, part) draws one part's arguments, and reference() takes and returns one part's arrays. A program takes and returns all parts, laid end to end along the dimension named above; each array names one. Nothing has to cross between parts.
Inputs may be any that keep to these rules, and one draw needn't show every extreme that they name: `owner_rank`: among the rows of one device, at most 128 particles name one owner, a bound that some block reaches.
All inputs are finite; a program needn't handle non-finite values. No bound on the sum of `active_block` on one device may be relied on, other than what follows from the above.
Results may differ from the reference program's by a relative error of at most 0.00002.
Values sent between devices are 32-bit elements; how exact they have to be, the bound alone decides.
A program may use at most 64 MiB of HBM per device.

```python
import math
import jax
import jax.numpy as jnp
import numpy as np

PD = 1024
BY = 4
BZ = 32
SWEEPS = 4
CAP = 128
BD = 256
PARTICLES = 16384
BLOCKS = 4096
GX = 128
GY = 16
GZ = 128
N_BLK = 16


def plant(result, stream_key, least, largest):
    dims = result.shape
    index_at = [jax.random.randint(jax.random.fold_in(stream_key, axis), (), 0, dims[axis]) for axis in range(len(dims))]
    result = result.at[tuple(index_at)].set(least)
    longest = dims.index(max(dims))
    index_at[longest] = (index_at[longest] + 1) % dims[longest]
    return result.at[tuple(index_at)].set(largest)


def shard_levels(key, shape, shards, low, largest):
    def one(position, parts):
        steps = jax.random.uniform(jax.random.fold_in(jax.random.fold_in(key, 6), position), (parts,), jnp.float32, low / len(shards), largest / len(shards))
        return jnp.repeat(jnp.exp(steps), shape[position] // parts).reshape((-1,) + (1,) * (len(shape) - position - 1))

    gain = one(*shards[0])
    for cut in shards[1:]:
        gain = gain * one(*cut)
    return gain


def assign_block(own_key, own, number, rows, count, top, limit, slope):
    ranking = jax.random.permutation(own_key, count)
    packed, common = shares(count, rows * top, limit, slope, True), shares(count, rows * top, limit, slope, False)
    places = jnp.arange(count)

    def named(sizes, offset_by):
        used = int((sizes > 0).sum())
        fixed = max(1, used // 4)
        passed = fixed + (places - fixed + offset_by * (used - fixed)) % max(1, count - fixed)
        return jnp.zeros((count,), jnp.int32).at[ranking[jnp.where(places < fixed, places, passed)]].set(jnp.asarray(sizes, jnp.int32))

    sizes = jnp.where(number % 4 == 0, named(packed, number // 4), named(common, number - number // 4 - 1))
    mixed = jax.random.permutation(jax.random.fold_in(own, 3), count)
    giver, sink = mixed[0:count // 2 * 2:2], mixed[1:count // 2 * 2:2]
    room = jnp.minimum(sizes[giver] - 1, limit - sizes[sink]) // 2
    room = jnp.where((giver == ranking[0]) | (sink == ranking[0]) | (sizes[sink] == 0), 0, jnp.maximum(room, 0))
    passed = jax.random.randint(jax.random.fold_in(own, 4), (count // 2,), 0, 1 << 20) % (room + 1)
    sizes = sizes.at[giver].add(-passed).at[sink].add(passed)
    items = jnp.searchsorted(jnp.cumsum(sizes), jnp.arange(rows * top), side="right").astype(jnp.int32)
    listing = items.reshape(top, rows).T
    listing = listing[jax.random.permutation(jax.random.fold_in(own, 1), rows)]
    offset_by = jax.random.randint(jax.random.fold_in(own, 2), (rows, 1), 0, top)
    return jnp.take_along_axis(listing, (jnp.arange(top)[None, :] + offset_by) % top, axis=1)


def shares(count, total, limit, lean, full):
    weights = [(1 << 20) // math.isqrt(standing ** lean) + 1 for standing in range(1, count + 1)]
    largest = limit if full else min(limit, max(-(-total // count), total * weights[0] // sum(weights)))
    least = 1 if total - largest >= count - 1 else 0
    counts, surplus = [largest] + [least] * (count - 1), total - largest - least * (count - 1)
    while surplus > 0:
        free = [i for i in range(1, count) if counts[i] < largest] or [i for i in range(1, count) if counts[i] < limit]
        pool, left = sum([weights[i] for i in free]), surplus
        for i in free:
            extra = min(limit - counts[i], max(1, left * weights[i] // pool), surplus)
            counts[i] = counts[i] + extra
            surplus = surplus - extra
    return np.array(counts)


def gaussian(key, extent, spread, most, pieces=(), kind=jnp.bfloat16):
    array = spread * jax.random.normal(key, extent, jnp.float32)
    if pieces:
        array = array * shard_levels(key, extent, pieces, -0.22, 0.18)
    return jnp.clip(array, -most, most).astype(kind)


def setup_inputs(seed: int = 0, part: int = 0) -> dict:
    splits = jax.random.split(jax.random.key(seed), 10)
    part_splits = jax.random.split(jax.random.fold_in(splits[9], part), 10)
    crack_energy = jnp.clip(jnp.exp(math.log(4.0) - 4.3820266 * jax.random.uniform(part_splits[0], (PARTICLES,), jnp.float32) ** shard_levels(part_splits[0], (PARTICLES,), ((0, 16),), -0.2, 0.2)), 0.05, 4.0)
    weights = jnp.clip(0.25 * jax.random.uniform(part_splits[1], (8, PARTICLES), jnp.float32) ** shard_levels(part_splits[1], (8, PARTICLES), ((1, 16),), -0.2, 0.2), 0.0, 0.25)
    elastic_stress = gaussian(part_splits[2], (6, PARTICLES), 1.0, 6.0, ((1, 16),), jnp.float32)
    owner_rank_keys = jax.random.split(jax.random.fold_in(part_splits[3], 1), PARTICLES // PD)
    owner_rank_turns = jax.random.permutation(jax.random.fold_in(part_splits[3], 3), PARTICLES // PD)
    owner_rank = jax.vmap(lambda own, number: assign_block(jax.random.fold_in(part_splits[3], 2), own, number, PD, N_BLK, 1, CAP, 2))(owner_rank_keys, owner_rank_turns).reshape((PARTICLES, 1))
    local_block = plant(jax.random.randint(part_splits[4], (PARTICLES,), 0, BD), jax.random.fold_in(part_splits[4], 1), 0, BD - 1).astype(jnp.int32)
    base_cell = plant(jax.random.randint(part_splits[5], (PARTICLES,), 0, 27), jax.random.fold_in(part_splits[5], 1), 0, 26).astype(jnp.int32)
    prior_damage = jnp.clip(0.6 * jax.random.uniform(part_splits[6], (GX, GY, GZ), jnp.float32) ** shard_levels(part_splits[6], (GX, GY, GZ), ((0, 16),), -0.2, 0.2), 0.0, 0.6)
    toughness = jnp.clip(jnp.exp(math.log(2.0) - 1.3862944 * jax.random.uniform(part_splits[7], (GX, GY, GZ), jnp.float32) ** shard_levels(part_splits[7], (GX, GY, GZ), ((0, 16),), -0.2, 0.2)), 0.5, 2.0)
    active_block = plant((jax.random.randint(part_splits[8], (BLOCKS,), 0, 4) < 3).astype(jnp.int32), jax.random.fold_in(part_splits[8], 1), 0, 1)
    return {"crack_energy": crack_energy, "weights": weights, "elastic_stress": elastic_stress, "owner_rank": owner_rank, "local_block": local_block, "base_cell": base_cell, "prior_damage": prior_damage, "toughness": toughness, "active_block": active_block}


length_scale = 2.0
stiff_floor = 0.001


def corner_offsets():
    corner = jnp.arange(8, dtype=jnp.int32)
    return corner // 4, (corner // 2) % 2, corner % 2


def cell_live(active_block, blocks_x):
    grid = active_block.reshape(blocks_x, BY, BZ).astype(jnp.float32)
    return jnp.repeat(jnp.repeat(jnp.repeat(grid, 4, 0), 4, 1), 4, 2)


def relax(extended, energy, toughness, live):
    padded = jnp.pad(extended, ((0, 0), (1, 1), (1, 1)))
    beside = padded[2:, 1:-1, 1:-1] + padded[:-2, 1:-1, 1:-1]
    beside = beside + padded[1:-1, 2:, 1:-1] + padded[1:-1, :-2, 1:-1]
    beside = beside + padded[1:-1, 1:-1, 2:] + padded[1:-1, 1:-1, :-2]
    couple = toughness * length_scale
    return live * (2.0 * energy + couple * beside) / (toughness / length_scale + 2.0 * energy + 6.0 * couple)


def reference(crack_energy, weights, elastic_stress, owner_rank, local_block, base_cell, prior_damage, toughness, active_block):
    size_x, size_y, size_z = prior_damage.shape
    slab_x = size_x // N_BLK
    target = owner_rank[:, 0]
    off_x, off_y, off_z = corner_offsets()
    block_x = local_block // (BY * BZ)
    block_y = (local_block // BZ) % BY
    block_z = local_block % BZ
    cell_x = (target * slab_x + 4 * block_x + base_cell // 9)[None, :] + off_x[:, None]
    cell_y = (4 * block_y + (base_cell // 3) % 3)[None, :] + off_y[:, None]
    cell_z = (4 * block_z + base_cell % 3)[None, :] + off_z[:, None]
    cell_index = ((cell_x * size_y + cell_y) * size_z + cell_z).astype(jnp.int32)
    terms = weights * crack_energy[None, :]
    energy = jnp.zeros((size_x * size_y * size_z,), jnp.float32).at[cell_index.ravel()].add(terms.ravel())
    energy = energy.reshape(size_x, size_y, size_z)
    live = cell_live(active_block, size_x // 4)
    damage = prior_damage
    for sweep in range(SWEEPS):
        damage = relax(jnp.pad(damage, ((1, 1), (0, 0), (0, 0))), energy, toughness, live)
    particle_damage = jnp.sum(weights * damage.ravel()[cell_index], axis=0)
    factor = (1.0 - particle_damage) ** 2 + stiff_floor
    return damage, factor[None, :] * elastic_stress
```

```python
import functools

import jax
import jax.numpy as jnp
from jax import lax
from jax.experimental import pallas as pl
from jax.experimental.pallas import tpu as pltpu
from jax.sharding import PartitionSpec as P

BY = 4
BZ = 32
SWEEPS = 4
LANES = 128
ROWS = 16

length_scale = 2.0
stiff_floor = 0.001

F32 = jnp.float32
BF16 = jnp.bfloat16


def iota(shape, axis):
    return lax.broadcasted_iota(jnp.int32, shape, axis)


def pieces(values):
    high = values.astype(BF16)
    rest = values - high.astype(F32)
    middle = rest.astype(BF16)
    low = (rest - middle.astype(F32)).astype(BF16)
    return high, middle, low


def dot_nt(left, right):
    return lax.dot_general(left, right, (((1,), (1,)), ((), ())), preferred_element_type=F32)


def dot_nn(left, right):
    return lax.dot_general(left, right, (((1,), (0,)), ((), ())), preferred_element_type=F32)


def loop(count, step, unrolled):
    if unrolled:
        for i in range(count):
            step(i)
    else:
        pl.loop(0, count)(step)


def kernel(
    n,
    size_x,
    size_y,
    energy_ref,
    weights_ref,
    stress_ref,
    owner_ref,
    block_ref,
    base_ref,
    prior_ref,
    tough_ref,
    active_ref,
    damage_ref,
    out_ref,
    send,
    arrived,
    mixed,
    zhot,
    total,
    energy_ext,
    tough_ext,
    prior_ext,
    back_send,
    back,
    send_sem,
    recv_sem,
    back_send_sem,
    back_recv_sem,
    side_send_sem,
    side_recv_sem,
):
    me = lax.axis_index("blk")
    cells = size_x * size_y
    count = owner_ref.shape[1]
    pad = SWEEPS * size_y
    inner = (SWEEPS - 1) * size_y
    unrolled = n <= 16

    def to(device):
        return {"blk": device}

    def side_copy(which, source, target, device):
        return pltpu.make_async_remote_copy(
            src_ref=source,
            dst_ref=target,
            send_sem=side_send_sem.at[which],
            recv_sem=side_recv_sem.at[which],
            device_id=to(device),
            device_id_type=pl.DeviceIdType.MESH,
        )

    def bucket_copy(device):
        return pltpu.make_async_remote_copy(
            src_ref=send.at[device],
            dst_ref=arrived.at[me],
            send_sem=send_sem.at[device],
            recv_sem=recv_sem.at[me],
            device_id=to(device),
            device_id_type=pl.DeviceIdType.MESH,
        )

    def bucket_arrival(device):
        return pltpu.make_async_remote_copy(
            src_ref=send.at[device],
            dst_ref=arrived.at[device],
            send_sem=send_sem.at[device],
            recv_sem=recv_sem.at[device],
            device_id=to(device),
            device_id_type=pl.DeviceIdType.MESH,
        )

    def back_copy(device):
        return pltpu.make_async_remote_copy(
            src_ref=back_send.at[device],
            dst_ref=back.at[me],
            send_sem=back_send_sem.at[device],
            recv_sem=back_recv_sem.at[me],
            device_id=to(device),
            device_id_type=pl.DeviceIdType.MESH,
        )

    def back_arrival(device):
        return pltpu.make_async_remote_copy(
            src_ref=back_send.at[device],
            dst_ref=back.at[device],
            send_sem=back_send_sem.at[device],
            recv_sem=back_recv_sem.at[device],
            device_id=to(device),
            device_id_type=pl.DeviceIdType.MESH,
        )

    for array in (energy_ext, tough_ext, prior_ext):
        array[:pad, :] = jnp.zeros((pad, LANES), F32)
        array[pad + cells :, :] = jnp.zeros((pad, LANES), F32)

    barrier = pltpu.get_barrier_semaphore()

    def greet(i):
        pl.semaphore_signal(
            barrier, inc=1, device_id=to(lax.rem(me + 1 + i, n)), device_id_type=pl.DeviceIdType.MESH
        )

    loop(n - 1, greet, unrolled)

    blocks = active_ref.shape[1]
    row, block = iota((cells, blocks), 0), iota((cells, blocks), 1)
    row_block = row // (4 * size_y) * BY + row % size_y // 4
    by_row = jnp.where(block // BZ == row_block, active_ref[...].astype(F32), 0.0).astype(BF16)
    by_lane = jnp.where(
        iota((LANES, blocks), 1) % BZ == iota((LANES, blocks), 0) // 4, 1.0, 0.0
    ).astype(BF16)
    live = dot_nt(by_row, by_lane)
    tough_ext[pad : pad + cells, :] = live * tough_ref[...]
    prior_ext[pad : pad + cells, :] = prior_ref[...]

    owner = owner_ref[...]
    owner_hot = jnp.where(iota((n, count), 0) == owner, 1.0, 0.0)
    chunks = count // LANES
    stacked = jnp.concatenate(
        [owner_hot[:, c * LANES : (c + 1) * LANES] for c in range(chunks)], axis=0
    ).astype(BF16)
    ahead = jnp.where(
        (iota((LANES, 2 * LANES), 0) < iota((LANES, 2 * LANES), 1))
        | (iota((LANES, 2 * LANES), 1) >= LANES),
        1.0,
        0.0,
    ).astype(BF16)
    counted = dot_nn(stacked, ahead)
    running = jnp.zeros((n, LANES), F32)
    places = []
    for c in range(chunks):
        part = counted[c * n : (c + 1) * n]
        hot = owner_hot[:, c * LANES : (c + 1) * LANES]
        places.append(jnp.sum(hot * (part[:, :LANES] + running), axis=0, keepdims=True))
        running = running + part[:, LANES:]
    place = jnp.concatenate(places, axis=1).astype(jnp.int32)
    place_hot = jnp.where(iota((LANES, count), 0) == place, 1.0, 0.0).astype(BF16)

    at_block, at_base = block_ref[...], base_ref[...]
    xy = (4 * (at_block // (BY * BZ)) + at_base // 9) * size_y
    xy = xy + 4 * (at_block // BZ % BY) + at_base // 3 % 3
    z = 4 * (at_block % BZ) + at_base % 3
    line = iota((8, count), 0)
    rest = jnp.where(
        line == 0,
        energy_ref[...],
        jnp.where(line == 1, xy.astype(F32), jnp.where(line == 2, z.astype(F32), 0.0)),
    )
    payload = jnp.concatenate(pieces(jnp.concatenate([weights_ref[...], rest], axis=0)), axis=0)
    group = min(n, 16)
    for first in range(0, n, group):
        chosen = []
        for device in range(first, first + group):
            mask = jnp.where(
                jnp.broadcast_to(owner, (3 * ROWS, count)) == device, 1.0, 0.0
            ).astype(BF16)
            chosen.append(payload * mask)
        bucket = dot_nt(jnp.concatenate(chosen, axis=0), place_hot)
        for i in range(group):
            part = bucket[3 * ROWS * i : 3 * ROWS * (i + 1)]
            send[first + i] = part[:ROWS] + part[ROWS : 2 * ROWS] + part[2 * ROWS :]

    pl.semaphore_wait(barrier, n - 1)

    loop(n - 1, lambda i: bucket_copy(lax.rem(me + 1 + i, n)).start(), unrolled)

    low, high = me > 0, me < n - 1
    end = pad + cells

    def upward(array, which, depth):
        return side_copy(
            which, array.at[pl.ds(end - depth, depth)], array.at[pl.ds(pad - depth, depth)], me + 1
        )

    def downward(array, which, depth):
        return side_copy(which, array.at[pl.ds(pad, depth)], array.at[pl.ds(end, depth)], me - 1)

    @pl.when(high)
    def _():
        upward(prior_ext, 0, pad).start()
        upward(tough_ext, 1, inner).start()

    @pl.when(low)
    def _():
        downward(prior_ext, 2, pad).start()
        downward(tough_ext, 3, inner).start()

    arrived[me] = send[me]
    total[...] = jnp.zeros_like(total)
    loop(n - 1, lambda i: bucket_arrival(lax.rem(me + n - 1 - i, n)).wait_recv(), unrolled)

    cell = iota((cells, LANES), 0)
    along = iota((LANES, LANES), 0)

    def gather_energy(pair):
        lefts, rights = [[], [], []], []
        for source in (2 * pair, 2 * pair + 1):
            rows = arrived[source]
            away = cell - rows[9:10].astype(jnp.int32)
            spread = []
            for k in range(2):
                spread.append(
                    jnp.where(
                        away == 0,
                        rows[k : k + 1],
                        jnp.where(
                            away == 1,
                            rows[k + 2 : k + 3],
                            jnp.where(
                                away == size_y,
                                rows[k + 4 : k + 5],
                                jnp.where(away == size_y + 1, rows[k + 6 : k + 7], 0.0),
                            ),
                        ),
                    )
                )
            spread = jnp.concatenate(spread, axis=0)
            mixed[source] = spread
            for held, piece in zip(lefts, pieces(spread * rows[8:9])):
                held.append(piece)
            hot = jnp.where(along == rows[10:11].astype(jnp.int32), 1.0, 0.0).astype(BF16)
            zhot[source] = hot
            rights.append(hot)
        left = jnp.concatenate(lefts[0] + lefts[1] + lefts[2], axis=1)
        total[...] += dot_nt(left, jnp.concatenate(rights * 3, axis=1))

    loop(n // 2, gather_energy, unrolled)
    energy_ext[pad:end, :] = total[:cells, :] + pltpu.roll(total[cells:, :], 1, 1)

    @pl.when(high)
    def _():
        upward(energy_ext, 4, inner).start()

    @pl.when(low)
    def _():
        downward(energy_ext, 5, inner).start()

    @pl.when(low)
    def _():
        upward(prior_ext, 0, pad).wait_recv()
        upward(tough_ext, 1, inner).wait_recv()
        upward(energy_ext, 4, inner).wait_recv()

    @pl.when(high)
    def _():
        downward(prior_ext, 2, pad).wait_recv()
        downward(tough_ext, 3, inner).wait_recv()
        downward(energy_ext, 5, inner).wait_recv()

    tough = tough_ext[...]
    twice = 2.0 * energy_ext[...]
    alive = tough > 0.0
    under = 1.0 / jnp.where(
        alive, twice + (1.0 / length_scale + 6.0 * length_scale) * tough, 1.0
    )
    couple = length_scale * tough * under
    source = jnp.where(alive, twice * under, 0.0)
    damage = prior_ext[...]
    rows = cells + 2 * pad
    row, lane = iota((rows, LANES), 0) % size_y, iota((rows, LANES), 1)
    blank = jnp.zeros((size_y, LANES), F32)
    for sweep in range(SWEEPS):
        beside = jnp.concatenate([damage[size_y:], blank], axis=0)
        beside = beside + jnp.concatenate([blank, damage[:-size_y]], axis=0)
        beside = beside + jnp.where(row == size_y - 1, 0.0, pltpu.roll(damage, rows - 1, 0))
        beside = beside + jnp.where(row == 0, 0.0, pltpu.roll(damage, 1, 0))
        beside = beside + jnp.where(lane == LANES - 1, 0.0, pltpu.roll(damage, LANES - 1, 1))
        beside = beside + jnp.where(lane == 0, 0.0, pltpu.roll(damage, 1, 1))
        damage = source + couple * beside
    damage = damage[pad:end]
    damage_ref[...] = damage

    both = jnp.concatenate([damage, pltpu.roll(damage, LANES - 1, 1)], axis=0)
    both = jnp.concatenate(pieces(both), axis=1)

    def sample(pair):
        hot = jnp.concatenate([zhot[2 * pair], zhot[2 * pair + 1]], axis=1)
        found = dot_nn(both, jnp.concatenate([hot] * 3, axis=0))
        for i in range(2):
            part = found[:, i * LANES : (i + 1) * LANES] * mixed[2 * pair + i]
            back_send[2 * pair + i] = jnp.sum(part, axis=0, keepdims=True)

    loop(n // 2, sample, unrolled)
    loop(n - 1, lambda i: back_copy(lax.rem(me + 1 + i, n)).start(), unrolled)
    back[me] = back_send[me]
    loop(n - 1, lambda i: back_arrival(lax.rem(me + n - 1 - i, n)).wait_recv(), unrolled)

    returned = jnp.concatenate([back[i] for i in range(n)], axis=0)
    found = dot_nn(jnp.concatenate(pieces(returned), axis=0), place_hot)
    found = found[:n] + found[n : 2 * n] + found[2 * n :]
    particle_damage = jnp.sum(found * owner_hot, axis=0, keepdims=True)
    factor = (1.0 - particle_damage) ** 2 + stiff_floor
    out_ref[...] = factor * stress_ref[...]

    def finish(i):
        device = lax.rem(me + 1 + i, n)
        bucket_copy(device).wait_send()
        back_copy(device).wait_send()

    loop(n - 1, finish, unrolled)

    @pl.when(high)
    def _():
        upward(prior_ext, 0, pad).wait_send()
        upward(tough_ext, 1, inner).wait_send()
        upward(energy_ext, 4, inner).wait_send()

    @pl.when(low)
    def _():
        downward(prior_ext, 2, pad).wait_send()
        downward(tough_ext, 3, inner).wait_send()
        downward(energy_ext, 5, inner).wait_send()


def body(
    crack_energy,
    weights,
    elastic_stress,
    owner_rank,
    local_block,
    base_cell,
    prior_damage,
    toughness,
    active_block,
):
    n = lax.axis_size("blk")
    count = crack_energy.shape[0]
    size_x, size_y, size_z = prior_damage.shape
    assert size_z == LANES and 2 * count // n <= LANES and size_x >= SWEEPS
    cells = size_x * size_y
    rows = cells + 2 * SWEEPS * size_y
    vmem = pl.BlockSpec(memory_space=pltpu.VMEM)
    damage, stress = pl.pallas_call(
        functools.partial(kernel, n, size_x, size_y),
        out_shape=(
            jax.ShapeDtypeStruct((cells, LANES), F32),
            jax.ShapeDtypeStruct(elastic_stress.shape, F32),
        ),
        in_specs=[vmem] * 9,
        out_specs=(vmem, vmem),
        scratch_shapes=[
            pltpu.VMEM((n, ROWS, LANES), F32),
            pltpu.VMEM((n, ROWS, LANES), F32),
            pltpu.VMEM((n, 2 * cells, LANES), F32),
            pltpu.VMEM((n, LANES, LANES), BF16),
            pltpu.VMEM((2 * cells, LANES), F32),
            pltpu.VMEM((rows, LANES), F32),
            pltpu.VMEM((rows, LANES), F32),
            pltpu.VMEM((rows, LANES), F32),
            pltpu.VMEM((n, 1, LANES), F32),
            pltpu.VMEM((n, 1, LANES), F32),
            pltpu.SemaphoreType.DMA((n,)),
            pltpu.SemaphoreType.DMA((n,)),
            pltpu.SemaphoreType.DMA((n,)),
            pltpu.SemaphoreType.DMA((n,)),
            pltpu.SemaphoreType.DMA((6,)),
            pltpu.SemaphoreType.DMA((6,)),
        ],
        compiler_params=pltpu.CompilerParams(
            collective_id=0,
            has_side_effects=True,
            vmem_limit_bytes=(24 if n <= 16 else 56) * 1024 * 1024,
        ),
    )(
        crack_energy.reshape(1, count),
        weights,
        elastic_stress,
        owner_rank.reshape(1, count),
        local_block.reshape(1, count),
        base_cell.reshape(1, count),
        prior_damage.reshape(cells, LANES),
        toughness.reshape(cells, LANES),
        active_block.reshape(1, active_block.shape[0]),
    )
    return (damage.reshape(prior_damage.shape), stress)


def solution(mesh):
    return jax.shard_map(
        body,
        mesh=mesh,
        in_specs=(
            P(("groups", "blk")),
            P(None, ("groups", "blk")),
            P(None, ("groups", "blk")),
            P(("groups", "blk"), None),
            P(("groups", "blk")),
            P(("groups", "blk")),
            P(("groups", "blk"), None, None),
            P(("groups", "blk"), None, None),
            P(("groups", "blk")),
        ),
        out_specs=(P(("groups", "blk"), None, None), P(None, ("groups", "blk"))),
        check_vma=False,
    )
```

```python
import functools

import jax
import jax.numpy as jnp
from jax import lax
from jax.experimental import pallas as pl
from jax.experimental.pallas import tpu as pltpu
from jax.sharding import PartitionSpec as P

BY = 4
BZ = 32
SWEEPS = 4
LANES = 128
ROWS = 16
USED = 10
GROUP = 4

length_scale = 2.0
stiff_floor = 0.001

F32 = jnp.float32
BF16 = jnp.bfloat16


def iota(shape, axis):
    return lax.broadcasted_iota(jnp.int32, shape, axis)


def pieces(values):
    high = values.astype(BF16)
    rest = values - high.astype(F32)
    middle = rest.astype(BF16)
    low = (rest - middle.astype(F32)).astype(BF16)
    return high, middle, low


def dot_nt(left, right):
    return lax.dot_general(left, right, (((1,), (1,)), ((), ())), preferred_element_type=F32)


def dot_nn(left, right):
    return lax.dot_general(left, right, (((1,), (0,)), ((), ())), preferred_element_type=F32)


def loop(count, step, unrolled):
    if unrolled:
        for i in range(count):
            step(i)
    else:
        pl.loop(0, count)(step)


def kernel(
    n,
    size_x,
    size_y,
    energy_in,
    weights_in,
    stress_in,
    owner_in,
    block_in,
    base_in,
    prior_in,
    tough_in,
    active_in,
    damage_ref,
    out_ref,
    energy_ref,
    weights_ref,
    stress_ref,
    owner_ref,
    block_ref,
    base_ref,
    tough_ref,
    active_ref,
    send,
    arrived,
    mixed,
    zhot,
    total,
    energy_ext,
    tough_ext,
    prior_ext,
    back_send,
    back,
    send_sem,
    recv_sem,
    back_send_sem,
    back_recv_sem,
    side_send_sem,
    side_recv_sem,
    load_sem,
):
    me = lax.axis_index("blk")
    cells = size_x * size_y
    count = owner_ref.shape[1]
    pad = SWEEPS * size_y
    loads = [
        pltpu.make_async_copy(source, target, load_sem.at[i])
        for i, (source, target) in enumerate(
            (
                (owner_in, owner_ref),
                (block_in, block_ref),
                (base_in, base_ref),
                (energy_in, energy_ref),
                (weights_in, weights_ref),
                (active_in, active_ref),
                (tough_in, tough_ref),
                (prior_in, prior_ext.at[pl.ds(pad, cells)]),
                (stress_in, stress_ref),
            )
        )
    ]
    for load in loads:
        load.start()
    inner = (SWEEPS - 1) * size_y
    unrolled = n <= 16

    def to(device):
        return {"blk": device}

    def side_copy(which, source, target, device):
        return pltpu.make_async_remote_copy(
            src_ref=source,
            dst_ref=target,
            send_sem=side_send_sem.at[which],
            recv_sem=side_recv_sem.at[which],
            device_id=to(device),
            device_id_type=pl.DeviceIdType.MESH,
        )

    def partner(i):
        device, bit = 0, 1
        while bit < n:
            mine = lax.rem(lax.div(me, jnp.int32(bit)), jnp.int32(2))
            if isinstance(i, int):
                mine = 1 - mine if i // bit % 2 else mine
            else:
                mine = lax.rem(mine + lax.div(i, jnp.int32(bit)), jnp.int32(2))
            device, bit = device + mine * bit, 2 * bit
        return device

    def swap(i, source, target, sends, receives):
        return pltpu.make_async_remote_copy(
            src_ref=source,
            dst_ref=target,
            send_sem=sends.at[i],
            recv_sem=receives.at[i],
            device_id=to(partner(i)),
            device_id_type=pl.DeviceIdType.MESH,
        )

    def bucket_copy(i):
        used = pl.ds(0, USED)
        return swap(i, send.at[i, used], arrived.at[i, used], send_sem, recv_sem)

    def back_copy(i):
        return swap(i, back_send.at[i], back.at[i], back_send_sem, back_recv_sem)

    for array in (energy_ext, tough_ext, prior_ext):
        array[:pad, :] = jnp.zeros((pad, LANES), F32)
        array[pad + cells :, :] = jnp.zeros((pad, LANES), F32)

    barrier = pltpu.get_barrier_semaphore()

    def greet(i):
        pl.semaphore_signal(
            barrier, inc=1, device_id=to(partner(i + 1)), device_id_type=pl.DeviceIdType.MESH
        )

    loop(n - 1, greet, unrolled)

    loads[0].wait()
    owner = jnp.bitwise_xor(owner_ref[...], me)
    owner_hot = jnp.where(iota((n, count), 0) == owner, 1.0, 0.0)
    chunks = count // LANES
    stacked = jnp.concatenate(
        [owner_hot[:, c * LANES : (c + 1) * LANES] for c in range(chunks)], axis=0
    ).astype(BF16)
    ahead = jnp.where(
        (iota((LANES, 2 * LANES), 0) < iota((LANES, 2 * LANES), 1))
        | (iota((LANES, 2 * LANES), 1) >= LANES),
        1.0,
        0.0,
    ).astype(BF16)
    counted = dot_nn(stacked, ahead)
    running = jnp.zeros((n, LANES), F32)
    places = []
    for c in range(chunks):
        part = counted[c * n : (c + 1) * n]
        hot = owner_hot[:, c * LANES : (c + 1) * LANES]
        places.append(jnp.sum(hot * (part[:, :LANES] + running), axis=0, keepdims=True))
        running = running + part[:, LANES:]
    place = jnp.concatenate(places, axis=1).astype(jnp.int32)
    place_hot = jnp.where(iota((LANES, count), 0) == place, 1.0, 0.0).astype(BF16)

    for load in loads[1:5]:
        load.wait()
    at_block, at_base = block_ref[...], base_ref[...]
    xy = (4 * (at_block // (BY * BZ)) + at_base // 9) * size_y
    xy = xy + 4 * (at_block // BZ % BY) + at_base // 3 % 3
    z = 4 * (at_block % BZ) + at_base % 3
    line = iota((8, count), 0)
    rest = jnp.where(
        line == 0,
        energy_ref[...],
        jnp.where(line == 1, (xy * LANES + z).astype(F32), 0.0),
    )
    payload = pieces(jnp.concatenate([weights_ref[...], rest], axis=0))
    wide_owner = jnp.broadcast_to(owner, (ROWS, count))

    def fill(group):
        first = n - GROUP - GROUP * group
        chosen = []
        for i in range(GROUP):
            mask = jnp.where(wide_owner == first + i, 1.0, 0.0).astype(BF16)
            chosen += [piece * mask for piece in payload]
        bucket = dot_nt(jnp.concatenate(chosen, axis=0), place_hot)
        for i in range(GROUP):
            part = bucket[3 * ROWS * i : 3 * ROWS * (i + 1)]
            send[first + i] = part[:ROWS] + part[ROWS : 2 * ROWS] + part[2 * ROWS :]
        return first

    def fill_and_send(group):
        first = fill(group)
        for i in range(GROUP):
            bucket_copy(first + i).start()

    loop(1, fill, True)
    pl.semaphore_wait(barrier, n - 1)
    for i in range(GROUP):
        bucket_copy(n - GROUP + i).start()
    loop(n // GROUP - 2, lambda group: fill_and_send(group + 1), unrolled)
    fill(n // GROUP - 1)
    for i in range(1, GROUP):
        bucket_copy(i).start()

    for load in loads[5:8]:
        load.wait()
    blocks = active_ref.shape[1]
    row, block = iota((cells, blocks), 0), iota((cells, blocks), 1)
    row_block = row // (4 * size_y) * BY + row % size_y // 4
    by_row = jnp.where(block // BZ == row_block, active_ref[...].astype(F32), 0.0).astype(BF16)
    by_lane = jnp.where(
        iota((LANES, blocks), 1) % BZ == iota((LANES, blocks), 0) // 4, 1.0, 0.0
    ).astype(BF16)
    live = dot_nt(by_row, by_lane)
    tough_ext[pad : pad + cells, :] = live * tough_ref[...]

    low, high = me > 0, me < n - 1
    end = pad + cells

    def upward(array, which, depth):
        return side_copy(
            which, array.at[pl.ds(end - depth, depth)], array.at[pl.ds(pad - depth, depth)], me + 1
        )

    def downward(array, which, depth):
        return side_copy(which, array.at[pl.ds(pad, depth)], array.at[pl.ds(end, depth)], me - 1)

    @pl.when(high)
    def _():
        upward(prior_ext, 0, pad).start()
        upward(tough_ext, 1, inner).start()

    @pl.when(low)
    def _():
        downward(prior_ext, 2, pad).start()
        downward(tough_ext, 3, inner).start()

    arrived[0] = send[0]
    total[...] = jnp.zeros_like(total)

    cell = iota((cells, LANES), 0)
    along = iota((LANES, LANES), 0)

    def gather_energy(group):
        lefts, rights = [[], [], []], []
        for i in range(GROUP):
            source = GROUP * group + i
            if not (isinstance(source, int) and source == 0):
                bucket_copy(source).wait_recv()
        for i in range(GROUP):
            source = GROUP * group + i
            rows, code = arrived[source, :8], arrived[source, 9:10].astype(jnp.int32)
            away = cell - code // LANES
            spread = []
            for k in range(2):
                spread.append(
                    jnp.where(
                        away == 0,
                        rows[k : k + 1],
                        jnp.where(
                            away == 1,
                            rows[k + 2 : k + 3],
                            jnp.where(
                                away == size_y,
                                rows[k + 4 : k + 5],
                                jnp.where(away == size_y + 1, rows[k + 6 : k + 7], 0.0),
                            ),
                        ),
                    )
                )
            spread = jnp.concatenate(spread, axis=0)
            mixed[source] = spread
            for held, piece in zip(lefts, pieces(spread * arrived[source, 8:9])):
                held.append(piece)
            hot = jnp.where(along == code % LANES, 1.0, 0.0).astype(BF16)
            zhot[source] = hot
            rights.append(hot)
        left = jnp.concatenate(lefts[0] + lefts[1] + lefts[2], axis=1)
        total[...] += dot_nt(left, jnp.concatenate(rights * 3, axis=1))

    gather_energy(0)
    loop(n // GROUP - 1, lambda group: gather_energy(group + 1), unrolled)
    energy_ext[pad:end, :] = total[:cells, :] + pltpu.roll(total[cells:, :], 1, 1)

    @pl.when(high)
    def _():
        upward(energy_ext, 4, inner).start()

    @pl.when(low)
    def _():
        downward(energy_ext, 5, inner).start()

    @pl.when(low)
    def _():
        upward(prior_ext, 0, pad).wait_recv()
        upward(tough_ext, 1, inner).wait_recv()
        upward(energy_ext, 4, inner).wait_recv()

    @pl.when(high)
    def _():
        downward(prior_ext, 2, pad).wait_recv()
        downward(tough_ext, 3, inner).wait_recv()
        downward(energy_ext, 5, inner).wait_recv()

    tough = tough_ext[...]
    twice = 2.0 * energy_ext[...]
    alive = tough > 0.0
    under = 1.0 / jnp.where(
        alive, twice + (1.0 / length_scale + 6.0 * length_scale) * tough, 1.0
    )
    couple = length_scale * tough * under
    source = jnp.where(alive, twice * under, 0.0)
    damage = prior_ext[...]
    rows = cells + 2 * pad
    row, lane = iota((rows, LANES), 0) % size_y, iota((rows, LANES), 1)
    blank = jnp.zeros((size_y, LANES), F32)
    for sweep in range(SWEEPS):
        beside = jnp.concatenate([damage[size_y:], blank], axis=0)
        beside = beside + jnp.concatenate([blank, damage[:-size_y]], axis=0)
        beside = beside + jnp.where(row == size_y - 1, 0.0, pltpu.roll(damage, rows - 1, 0))
        beside = beside + jnp.where(row == 0, 0.0, pltpu.roll(damage, 1, 0))
        beside = beside + jnp.where(lane == LANES - 1, 0.0, pltpu.roll(damage, LANES - 1, 1))
        beside = beside + jnp.where(lane == 0, 0.0, pltpu.roll(damage, 1, 1))
        damage = source + couple * beside
    damage = damage[pad:end]
    damage_ref[...] = damage

    both = jnp.concatenate([damage, pltpu.roll(damage, LANES - 1, 1)], axis=0)
    both = jnp.concatenate(pieces(both), axis=1)

    def sample(step):
        first = n - 2 - 2 * step
        hot = jnp.concatenate([zhot[first], zhot[first + 1]], axis=1)
        found = dot_nn(both, jnp.concatenate([hot] * 3, axis=0))
        for i in range(2):
            part = found[:, i * LANES : (i + 1) * LANES] * mixed[first + i]
            back_send[first + i] = jnp.sum(part, axis=0, keepdims=True)

    def sample_and_send(step):
        sample(step)
        back_copy(n - 2 - 2 * step).start()
        back_copy(n - 1 - 2 * step).start()

    loop(n // 2 - 1, sample_and_send, unrolled)
    sample(n // 2 - 1)
    back_copy(1).start()
    back[0] = back_send[0]
    loop(n - 1, lambda i: back_copy(i + 1).wait_recv(), unrolled)

    returned = jnp.concatenate([back[i] for i in range(n)], axis=0)
    found = dot_nn(jnp.concatenate(pieces(returned), axis=0), place_hot)
    found = found[:n] + found[n : 2 * n] + found[2 * n :]
    particle_damage = jnp.sum(found * owner_hot, axis=0, keepdims=True)
    factor = (1.0 - particle_damage) ** 2 + stiff_floor
    loads[8].wait()
    out_ref[...] = factor * stress_ref[...]

    def finish(i):
        bucket_copy(i + 1).wait_send()
        back_copy(i + 1).wait_send()

    loop(n - 1, finish, unrolled)

    @pl.when(high)
    def _():
        upward(prior_ext, 0, pad).wait_send()
        upward(tough_ext, 1, inner).wait_send()
        upward(energy_ext, 4, inner).wait_send()

    @pl.when(low)
    def _():
        downward(prior_ext, 2, pad).wait_send()
        downward(tough_ext, 3, inner).wait_send()
        downward(energy_ext, 5, inner).wait_send()


def body(
    crack_energy,
    weights,
    elastic_stress,
    owner_rank,
    local_block,
    base_cell,
    prior_damage,
    toughness,
    active_block,
):
    n = lax.axis_size("blk")
    count = crack_energy.shape[0]
    size_x, size_y, size_z = prior_damage.shape
    assert n >= 2 * GROUP and n & (n - 1) == 0
    assert size_z == LANES and 2 * count // n <= LANES and size_x >= SWEEPS
    cells = size_x * size_y
    rows = cells + 2 * SWEEPS * size_y
    vmem = pl.BlockSpec(memory_space=pltpu.VMEM)
    damage, stress = pl.pallas_call(
        functools.partial(kernel, n, size_x, size_y),
        out_shape=(
            jax.ShapeDtypeStruct((cells, LANES), F32),
            jax.ShapeDtypeStruct(elastic_stress.shape, F32),
        ),
        in_specs=[pl.BlockSpec(memory_space=pltpu.HBM)] * 9,
        out_specs=(vmem, vmem),
        scratch_shapes=[
            pltpu.VMEM((1, count), F32),
            pltpu.VMEM(weights.shape, F32),
            pltpu.VMEM(elastic_stress.shape, F32),
            pltpu.VMEM((1, count), jnp.int32),
            pltpu.VMEM((1, count), jnp.int32),
            pltpu.VMEM((1, count), jnp.int32),
            pltpu.VMEM((cells, LANES), F32),
            pltpu.VMEM((1, active_block.shape[0]), jnp.int32),
            pltpu.VMEM((n, ROWS, LANES), F32),
            pltpu.VMEM((n, ROWS, LANES), F32),
            pltpu.VMEM((n, 2 * cells, LANES), F32),
            pltpu.VMEM((n, LANES, LANES), BF16),
            pltpu.VMEM((2 * cells, LANES), F32),
            pltpu.VMEM((rows, LANES), F32),
            pltpu.VMEM((rows, LANES), F32),
            pltpu.VMEM((rows, LANES), F32),
            pltpu.VMEM((n, 1, LANES), F32),
            pltpu.VMEM((n, 1, LANES), F32),
            pltpu.SemaphoreType.DMA((n,)),
            pltpu.SemaphoreType.DMA((n,)),
            pltpu.SemaphoreType.DMA((n,)),
            pltpu.SemaphoreType.DMA((n,)),
            pltpu.SemaphoreType.DMA((6,)),
            pltpu.SemaphoreType.DMA((6,)),
            pltpu.SemaphoreType.DMA((9,)),
        ],
        compiler_params=pltpu.CompilerParams(
            collective_id=0,
            has_side_effects=True,
            vmem_limit_bytes=60 * 1024 * 1024,
        ),
    )(
        crack_energy.reshape(1, count),
        weights,
        elastic_stress,
        owner_rank.reshape(1, count),
        local_block.reshape(1, count),
        base_cell.reshape(1, count),
        prior_damage.reshape(cells, LANES),
        toughness.reshape(cells, LANES),
        active_block.reshape(1, active_block.shape[0]),
    )
    return (damage.reshape(prior_damage.shape), stress)


def solution(mesh):
    return jax.shard_map(
        body,
        mesh=mesh,
        in_specs=(
            P(("groups", "blk")),
            P(None, ("groups", "blk")),
            P(None, ("groups", "blk")),
            P(("groups", "blk"), None),
            P(("groups", "blk")),
            P(("groups", "blk")),
            P(("groups", "blk"), None, None),
            P(("groups", "blk"), None, None),
            P(("groups", "blk")),
        ),
        out_specs=(P(("groups", "blk"), None, None), P(None, ("groups", "blk"))),
        check_vma=False,
    )
```

```python
import functools

import jax
import jax.numpy as jnp
from jax import lax
from jax.experimental import pallas as pl
from jax.experimental.pallas import tpu as pltpu
from jax.sharding import PartitionSpec as P

BY = 4
BZ = 32
SWEEPS = 4
LANES = 128
ROWS = 16
USED = 10
GROUP = 4

length_scale = 2.0
stiff_floor = 0.001

F32 = jnp.float32
BF16 = jnp.bfloat16


def iota(shape, axis):
    return lax.broadcasted_iota(jnp.int32, shape, axis)


def pieces(values):
    high = values.astype(BF16)
    rest = values - high.astype(F32)
    middle = rest.astype(BF16)
    low = (rest - middle.astype(F32)).astype(BF16)
    return high, middle, low


def dot_nt(left, right):
    return lax.dot_general(left, right, (((1,), (1,)), ((), ())), preferred_element_type=F32)


def dot_nn(left, right):
    return lax.dot_general(left, right, (((1,), (0,)), ((), ())), preferred_element_type=F32)


def loop(count, step, unrolled):
    if unrolled:
        for i in range(count):
            step(i)
    else:
        pl.loop(0, count)(step)


def kernel(
    n,
    size_x,
    size_y,
    energy_in,
    weights_in,
    stress_in,
    owner_in,
    block_in,
    base_in,
    prior_in,
    tough_in,
    active_in,
    damage_ref,
    out_ref,
    energy_ref,
    weights_ref,
    stress_ref,
    owner_ref,
    block_ref,
    base_ref,
    tough_ref,
    active_ref,
    send,
    arrived,
    mixed,
    zhot,
    total,
    energy_ext,
    tough_ext,
    prior_ext,
    back_send,
    back,
    send_sem,
    recv_sem,
    back_send_sem,
    back_recv_sem,
    side_send_sem,
    side_recv_sem,
    load_sem,
):
    me = lax.axis_index("blk")
    cells = size_x * size_y
    count = owner_ref.shape[1]
    pad = SWEEPS * size_y
    loads = [
        pltpu.make_async_copy(source, target, load_sem.at[i])
        for i, (source, target) in enumerate(
            (
                (owner_in, owner_ref),
                (block_in, block_ref),
                (base_in, base_ref),
                (energy_in, energy_ref),
                (weights_in, weights_ref),
                (active_in, active_ref),
                (tough_in, tough_ref),
                (prior_in, prior_ext.at[pl.ds(pad, cells)]),
                (stress_in, stress_ref),
            )
        )
    ]
    for load in loads:
        load.start()
    inner = (SWEEPS - 1) * size_y
    unrolled = n <= 16

    def to(device):
        return {"blk": device}

    def side_copy(which, source, target, device):
        return pltpu.make_async_remote_copy(
            src_ref=source,
            dst_ref=target,
            send_sem=side_send_sem.at[which],
            recv_sem=side_recv_sem.at[which],
            device_id=to(device),
            device_id_type=pl.DeviceIdType.MESH,
        )

    def partner(i):
        device, bit = 0, 1
        while bit < n:
            mine = lax.rem(lax.div(me, jnp.int32(bit)), jnp.int32(2))
            if isinstance(i, int):
                mine = 1 - mine if i // bit % 2 else mine
            else:
                mine = lax.rem(mine + lax.div(i, jnp.int32(bit)), jnp.int32(2))
            device, bit = device + mine * bit, 2 * bit
        return device

    def swap(i, source, target, sends, receives):
        return pltpu.make_async_remote_copy(
            src_ref=source,
            dst_ref=target,
            send_sem=sends.at[i],
            recv_sem=receives.at[i],
            device_id=to(partner(i)),
            device_id_type=pl.DeviceIdType.MESH,
        )

    def bucket_copy(i):
        used = pl.ds(0, USED)
        return swap(i, send.at[i, used], arrived.at[i, used], send_sem, recv_sem)

    def back_copy(i):
        return swap(i, back_send.at[i], back.at[i], back_send_sem, back_recv_sem)

    for array in (energy_ext, tough_ext, prior_ext):
        array[:pad, :] = jnp.zeros((pad, LANES), F32)
        array[pad + cells :, :] = jnp.zeros((pad, LANES), F32)

    barrier = pltpu.get_barrier_semaphore()

    def greet(i):
        pl.semaphore_signal(
            barrier, inc=1, device_id=to(partner(i + 1)), device_id_type=pl.DeviceIdType.MESH
        )

    loop(n - 1, greet, unrolled)

    loads[0].wait()
    owner = jnp.bitwise_xor(owner_ref[...], me)
    owner_hot = jnp.where(iota((n, count), 0) == owner, 1.0, 0.0)
    chunks = count // LANES
    stacked = jnp.concatenate(
        [owner_hot[:, c * LANES : (c + 1) * LANES] for c in range(chunks)], axis=0
    ).astype(BF16)
    ahead = jnp.where(
        (iota((LANES, 2 * LANES), 0) < iota((LANES, 2 * LANES), 1))
        | (iota((LANES, 2 * LANES), 1) >= LANES),
        1.0,
        0.0,
    ).astype(BF16)
    counted = dot_nn(stacked, ahead)
    running = jnp.zeros((n, LANES), F32)
    places = []
    for c in range(chunks):
        part = counted[c * n : (c + 1) * n]
        hot = owner_hot[:, c * LANES : (c + 1) * LANES]
        places.append(jnp.sum(hot * (part[:, :LANES] + running), axis=0, keepdims=True))
        running = running + part[:, LANES:]
    place = jnp.concatenate(places, axis=1).astype(jnp.int32)
    place_hot = jnp.where(iota((LANES, count), 0) == place, 1.0, 0.0).astype(BF16)

    for load in loads[1:5]:
        load.wait()
    at_block, at_base = block_ref[...], base_ref[...]
    xy = (4 * (at_block // (BY * BZ)) + at_base // 9) * size_y
    xy = xy + 4 * (at_block // BZ % BY) + at_base // 3 % 3
    z = 4 * (at_block % BZ) + at_base % 3
    line = iota((8, count), 0)
    rest = jnp.where(
        line == 0,
        energy_ref[...],
        jnp.where(line == 1, (xy * LANES + z).astype(F32), 0.0),
    )
    payload = pieces(jnp.concatenate([weights_ref[...], rest], axis=0))
    wide_owner = jnp.broadcast_to(owner, (ROWS, count))

    def fill(group):
        first = n - GROUP - GROUP * group
        chosen = []
        for i in range(GROUP):
            mask = jnp.where(wide_owner == first + i, 1.0, 0.0).astype(BF16)
            chosen += [piece * mask for piece in payload]
        bucket = dot_nt(jnp.concatenate(chosen, axis=0), place_hot)
        for i in range(GROUP):
            part = bucket[3 * ROWS * i : 3 * ROWS * (i + 1)]
            send[first + i] = part[:ROWS] + part[ROWS : 2 * ROWS] + part[2 * ROWS :]
        return first

    def fill_and_send(group):
        first = fill(group)
        for i in range(GROUP):
            bucket_copy(first + i).start()

    loop(1, fill, True)
    pl.semaphore_wait(barrier, n - 1)
    for i in range(GROUP):
        bucket_copy(n - GROUP + i).start()
    loop(n // GROUP - 2, lambda group: fill_and_send(group + 1), unrolled)
    fill(n // GROUP - 1)
    for i in range(1, GROUP):
        bucket_copy(i).start()

    for load in loads[5:8]:
        load.wait()
    blocks = active_ref.shape[1]
    row, block = iota((cells, blocks), 0), iota((cells, blocks), 1)
    row_block = row // (4 * size_y) * BY + row % size_y // 4
    by_row = jnp.where(block // BZ == row_block, active_ref[...].astype(F32), 0.0).astype(BF16)
    by_lane = jnp.where(
        iota((LANES, blocks), 1) % BZ == iota((LANES, blocks), 0) // 4, 1.0, 0.0
    ).astype(BF16)
    live = dot_nt(by_row, by_lane)
    tough_ext[pad : pad + cells, :] = live * tough_ref[...]

    low, high = me > 0, me < n - 1
    end = pad + cells

    def upward(array, which, depth):
        return side_copy(
            which, array.at[pl.ds(end - depth, depth)], array.at[pl.ds(pad - depth, depth)], me + 1
        )

    def downward(array, which, depth):
        return side_copy(which, array.at[pl.ds(pad, depth)], array.at[pl.ds(end, depth)], me - 1)

    @pl.when(high)
    def _():
        upward(prior_ext, 0, pad).start()
        upward(tough_ext, 1, inner).start()

    @pl.when(low)
    def _():
        downward(prior_ext, 2, pad).start()
        downward(tough_ext, 3, inner).start()

    arrived[0] = send[0]
    total[...] = jnp.zeros_like(total)

    cell = iota((cells, LANES), 0)
    along = iota((LANES, LANES), 0)

    def gather_energy(group):
        lefts, rights = [[], [], []], []
        for i in range(GROUP):
            source = GROUP * group + i
            if not (isinstance(source, int) and source == 0):
                bucket_copy(source).wait_recv()
        for i in range(GROUP):
            source = GROUP * group + i
            rows, code = arrived[source, :8], arrived[source, 9:10].astype(jnp.int32)
            away = cell - code // LANES
            spread = []
            for k in range(2):
                spread.append(
                    jnp.where(
                        away == 0,
                        rows[k : k + 1],
                        jnp.where(
                            away == 1,
                            rows[k + 2 : k + 3],
                            jnp.where(
                                away == size_y,
                                rows[k + 4 : k + 5],
                                jnp.where(away == size_y + 1, rows[k + 6 : k + 7], 0.0),
                            ),
                        ),
                    )
                )
            spread = jnp.concatenate(spread, axis=0)
            mixed[source] = spread
            for held, piece in zip(lefts, pieces(spread * arrived[source, 8:9])):
                held.append(piece)
            hot = jnp.where(along == code % LANES, 1.0, 0.0).astype(BF16)
            zhot[source] = hot
            rights.append(hot)
        left = jnp.concatenate(lefts[0] + lefts[1] + lefts[2], axis=1)
        total[...] += dot_nt(left, jnp.concatenate(rights * 3, axis=1))

    gather_energy(0)
    loop(n // GROUP - 1, lambda group: gather_energy(group + 1), unrolled)
    energy_ext[pad:end, :] = total[:cells, :] + pltpu.roll(total[cells:, :], 1, 1)

    @pl.when(high)
    def _():
        upward(energy_ext, 4, inner).start()

    @pl.when(low)
    def _():
        downward(energy_ext, 5, inner).start()

    @pl.when(low)
    def _():
        upward(prior_ext, 0, pad).wait_recv()
        upward(tough_ext, 1, inner).wait_recv()
        upward(energy_ext, 4, inner).wait_recv()

    @pl.when(high)
    def _():
        downward(prior_ext, 2, pad).wait_recv()
        downward(tough_ext, 3, inner).wait_recv()
        downward(energy_ext, 5, inner).wait_recv()

    tough = tough_ext[...]
    twice = 2.0 * energy_ext[...]
    alive = tough > 0.0
    under = 1.0 / jnp.where(
        alive, twice + (1.0 / length_scale + 6.0 * length_scale) * tough, 1.0
    )
    couple = length_scale * tough * under
    source = jnp.where(alive, twice * under, 0.0)
    damage = prior_ext[...]
    rows = cells + 2 * pad
    row, lane = iota((rows, LANES), 0) % size_y, iota((rows, LANES), 1)
    blank = jnp.zeros((size_y, LANES), F32)
    for sweep in range(SWEEPS):
        beside = jnp.concatenate([damage[size_y:], blank], axis=0)
        beside = beside + jnp.concatenate([blank, damage[:-size_y]], axis=0)
        beside = beside + jnp.where(row == size_y - 1, 0.0, pltpu.roll(damage, rows - 1, 0))
        beside = beside + jnp.where(row == 0, 0.0, pltpu.roll(damage, 1, 0))
        beside = beside + jnp.where(lane == LANES - 1, 0.0, pltpu.roll(damage, LANES - 1, 1))
        beside = beside + jnp.where(lane == 0, 0.0, pltpu.roll(damage, 1, 1))
        damage = source + couple * beside
    damage = damage[pad:end]
    damage_ref[...] = damage

    both = jnp.concatenate([damage, pltpu.roll(damage, LANES - 1, 1)], axis=0)
    both = jnp.concatenate(pieces(both), axis=1)

    def sample(step):
        first = n - 2 - 2 * step
        hot = jnp.concatenate([zhot[first], zhot[first + 1]], axis=1)
        found = dot_nn(both, jnp.concatenate([hot] * 3, axis=0))
        for i in range(2):
            part = found[:, i * LANES : (i + 1) * LANES] * mixed[first + i]
            back_send[first + i] = jnp.sum(part, axis=0, keepdims=True)

    def sample_and_send(step):
        sample(step)
        back_copy(n - 2 - 2 * step).start()
        back_copy(n - 1 - 2 * step).start()

    loop(n // 2 - 1, sample_and_send, unrolled)
    sample(n // 2 - 1)
    back_copy(1).start()
    back[0] = back_send[0]
    loop(n - 1, lambda i: back_copy(i + 1).wait_recv(), unrolled)

    returned = jnp.concatenate([back[i] for i in range(n)], axis=0)
    found = dot_nn(jnp.concatenate(pieces(returned), axis=0), place_hot)
    found = found[:n] + found[n : 2 * n] + found[2 * n :]
    particle_damage = jnp.sum(found * owner_hot, axis=0, keepdims=True)
    factor = (1.0 - particle_damage) ** 2 + stiff_floor
    loads[8].wait()
    out_ref[...] = factor * stress_ref[...]

    def finish(i):
        bucket_copy(i + 1).wait_send()
        back_copy(i + 1).wait_send()

    loop(n - 1, finish, unrolled)

    @pl.when(high)
    def _():
        upward(prior_ext, 0, pad).wait_send()
        upward(tough_ext, 1, inner).wait_send()
        upward(energy_ext, 4, inner).wait_send()

    @pl.when(low)
    def _():
        downward(prior_ext, 2, pad).wait_send()
        downward(tough_ext, 3, inner).wait_send()
        downward(energy_ext, 5, inner).wait_send()


def body(
    crack_energy,
    weights,
    elastic_stress,
    owner_rank,
    local_block,
    base_cell,
    prior_damage,
    toughness,
    active_block,
):
    n = lax.axis_size("blk")
    count = crack_energy.shape[0]
    size_x, size_y, size_z = prior_damage.shape
    assert n >= 2 * GROUP and n & (n - 1) == 0
    assert size_z == LANES and 2 * count // n <= LANES and size_x >= SWEEPS
    cells = size_x * size_y
    rows = cells + 2 * SWEEPS * size_y
    vmem = pl.BlockSpec(memory_space=pltpu.VMEM)
    damage, stress = pl.pallas_call(
        functools.partial(kernel, n, size_x, size_y),
        out_shape=(
            pltpu.VMEM((cells, LANES), F32),
            pltpu.VMEM(elastic_stress.shape, F32),
        ),
        in_specs=[pl.BlockSpec(memory_space=pltpu.HBM)] * 9,
        out_specs=(vmem, vmem),
        scratch_shapes=[
            pltpu.VMEM((1, count), F32),
            pltpu.VMEM(weights.shape, F32),
            pltpu.VMEM(elastic_stress.shape, F32),
            pltpu.VMEM((1, count), jnp.int32),
            pltpu.VMEM((1, count), jnp.int32),
            pltpu.VMEM((1, count), jnp.int32),
            pltpu.VMEM((cells, LANES), F32),
            pltpu.VMEM((1, active_block.shape[0]), jnp.int32),
            pltpu.VMEM((n, ROWS, LANES), F32),
            pltpu.VMEM((n, ROWS, LANES), F32),
            pltpu.VMEM((n, 2 * cells, LANES), F32),
            pltpu.VMEM((n, LANES, LANES), BF16),
            pltpu.VMEM((2 * cells, LANES), F32),
            pltpu.VMEM((rows, LANES), F32),
            pltpu.VMEM((rows, LANES), F32),
            pltpu.VMEM((rows, LANES), F32),
            pltpu.VMEM((n, 1, LANES), F32),
            pltpu.VMEM((n, 1, LANES), F32),
            pltpu.SemaphoreType.DMA((n,)),
            pltpu.SemaphoreType.DMA((n,)),
            pltpu.SemaphoreType.DMA((n,)),
            pltpu.SemaphoreType.DMA((n,)),
            pltpu.SemaphoreType.DMA((6,)),
            pltpu.SemaphoreType.DMA((6,)),
            pltpu.SemaphoreType.DMA((9,)),
        ],
        compiler_params=pltpu.CompilerParams(
            collective_id=0,
            has_side_effects=True,
            vmem_limit_bytes=60 * 1024 * 1024,
        ),
    )(
        crack_energy.reshape(1, count),
        weights,
        elastic_stress,
        owner_rank.reshape(1, count),
        local_block.reshape(1, count),
        base_cell.reshape(1, count),
        prior_damage.reshape(cells, LANES),
        toughness.reshape(cells, LANES),
        active_block.reshape(1, active_block.shape[0]),
    )
    return (damage.reshape(prior_damage.shape), stress)


def solution(mesh):
    return jax.shard_map(
        body,
        mesh=mesh,
        in_specs=(
            P(("groups", "blk")),
            P(None, ("groups", "blk")),
            P(None, ("groups", "blk")),
            P(("groups", "blk"), None),
            P(("groups", "blk")),
            P(("groups", "blk")),
            P(("groups", "blk"), None, None),
            P(("groups", "blk"), None, None),
            P(("groups", "blk")),
        ),
        out_specs=(P(("groups", "blk"), None, None), P(None, ("groups", "blk"))),
        check_vma=False,
    )
```

```python
import functools

import jax
import jax.numpy as jnp
from jax import lax
from jax.experimental import pallas as pl
from jax.experimental.pallas import tpu as pltpu
from jax.sharding import PartitionSpec as P

BY = 4
BZ = 32
SWEEPS = 4
LANES = 128
ROWS = 16
USED = 10
GROUP = 4

length_scale = 2.0
stiff_floor = 0.001

F32 = jnp.float32
BF16 = jnp.bfloat16


def iota(shape, axis):
    return lax.broadcasted_iota(jnp.int32, shape, axis)


def pieces(values):
    high = values.astype(BF16)
    rest = values - high.astype(F32)
    middle = rest.astype(BF16)
    low = (rest - middle.astype(F32)).astype(BF16)
    return high, middle, low


def dot_nt(left, right):
    return lax.dot_general(left, right, (((1,), (1,)), ((), ())), preferred_element_type=F32)


def dot_nn(left, right):
    return lax.dot_general(left, right, (((1,), (0,)), ((), ())), preferred_element_type=F32)


def loop(count, step, unrolled):
    if unrolled:
        for i in range(count):
            step(i)
    else:

        @pl.loop(0, count)
        def _(i):
            step(i)


def kernel(
    n,
    size_x,
    size_y,
    energy_in,
    weights_in,
    stress_in,
    owner_in,
    block_in,
    base_in,
    prior_in,
    tough_in,
    active_in,
    damage_ref,
    out_ref,
    energy_ref,
    weights_ref,
    stress_ref,
    owner_ref,
    block_ref,
    base_ref,
    tough_ref,
    active_ref,
    send,
    arrived,
    mixed,
    zhot,
    total,
    energy_ext,
    tough_ext,
    prior_ext,
    back_send,
    back,
    send_sem,
    recv_sem,
    back_send_sem,
    back_recv_sem,
    side_send_sem,
    side_recv_sem,
    load_sem,
):
    me = lax.axis_index("blk")
    cells = size_x * size_y
    count = owner_ref.shape[1]
    pad = SWEEPS * size_y
    loads = [
        pltpu.make_async_copy(source, target, load_sem.at[i])
        for i, (source, target) in enumerate(
            (
                (owner_in, owner_ref),
                (block_in, block_ref),
                (base_in, base_ref),
                (energy_in, energy_ref),
                (weights_in, weights_ref),
                (active_in, active_ref),
                (tough_in, tough_ref),
                (prior_in, prior_ext.at[pl.ds(pad, cells)]),
                (stress_in, stress_ref),
            )
        )
    ]
    for load in loads:
        load.start()
    inner = (SWEEPS - 1) * size_y
    unrolled = n <= 16

    def to(device):
        return {"blk": device}

    def side_copy(which, source, target, device):
        return pltpu.make_async_remote_copy(
            src_ref=source,
            dst_ref=target,
            send_sem=side_send_sem.at[which],
            recv_sem=side_recv_sem.at[which],
            device_id=to(device),
            device_id_type=pl.DeviceIdType.MESH,
        )

    def partner(i):
        device, bit = 0, 1
        while bit < n:
            mine = lax.rem(lax.div(me, jnp.int32(bit)), jnp.int32(2))
            if isinstance(i, int):
                mine = 1 - mine if i // bit % 2 else mine
            else:
                mine = lax.rem(mine + lax.div(i, jnp.int32(bit)), jnp.int32(2))
            device, bit = device + mine * bit, 2 * bit
        return device

    def swap(i, source, target, sends, receives):
        return pltpu.make_async_remote_copy(
            src_ref=source,
            dst_ref=target,
            send_sem=sends.at[i],
            recv_sem=receives.at[i],
            device_id=to(partner(i)),
            device_id_type=pl.DeviceIdType.MESH,
        )

    def bucket_copy(i):
        used = pl.ds(0, USED)
        return swap(i, send.at[i, used], arrived.at[i, used], send_sem, recv_sem)

    def back_copy(i):
        return swap(i, back_send.at[i], back.at[i], back_send_sem, back_recv_sem)

    for array in (energy_ext, tough_ext, prior_ext):
        array[:pad, :] = jnp.zeros((pad, LANES), F32)
        array[pad + cells :, :] = jnp.zeros((pad, LANES), F32)

    barrier = pltpu.get_barrier_semaphore()

    def greet(i):
        pl.semaphore_signal(
            barrier, inc=1, device_id=to(partner(i + 1)), device_id_type=pl.DeviceIdType.MESH
        )

    loop(n - 1, greet, unrolled)

    for load in loads[:5]:
        load.wait()
    owner = jnp.bitwise_xor(owner_ref[...], me)
    owner_hot = jnp.where(iota((n, count), 0) == owner, 1.0, 0.0)
    chunks = count // LANES
    stacked = jnp.concatenate(
        [owner_hot[:, c * LANES : (c + 1) * LANES] for c in range(chunks)], axis=0
    ).astype(BF16)
    ahead = jnp.where(
        (iota((LANES, 2 * LANES), 0) < iota((LANES, 2 * LANES), 1))
        | (iota((LANES, 2 * LANES), 1) >= LANES),
        1.0,
        0.0,
    ).astype(BF16)
    counted = dot_nn(stacked, ahead)
    running = jnp.zeros((n, LANES), F32)
    places = []
    for c in range(chunks):
        part = counted[c * n : (c + 1) * n]
        hot = owner_hot[:, c * LANES : (c + 1) * LANES]
        places.append(jnp.sum(hot * (part[:, :LANES] + running), axis=0, keepdims=True))
        running = running + part[:, LANES:]
    place = jnp.concatenate(places, axis=1).astype(jnp.int32)
    place_hot = jnp.where(iota((LANES, count), 0) == place, 1.0, 0.0).astype(BF16)

    at_block, at_base = block_ref[...], base_ref[...]
    xy = (4 * (at_block // (BY * BZ)) + at_base // 9) * size_y
    xy = xy + 4 * (at_block // BZ % BY) + at_base // 3 % 3
    z = 4 * (at_block % BZ) + at_base % 3
    line = iota((8, count), 0)
    rest = jnp.where(
        line == 0,
        energy_ref[...],
        jnp.where(line == 1, (xy * LANES + z).astype(F32), 0.0),
    )
    payload = pieces(jnp.concatenate([weights_ref[...], rest], axis=0))
    wide_owner = jnp.broadcast_to(owner, (ROWS, count))

    def fill(group):
        first = n - GROUP - GROUP * group
        chosen = []
        for i in range(GROUP):
            mask = jnp.where(wide_owner == first + i, 1.0, 0.0).astype(BF16)
            chosen += [piece * mask for piece in payload]
        bucket = dot_nt(jnp.concatenate(chosen, axis=0), place_hot)
        for i in range(GROUP):
            part = bucket[3 * ROWS * i : 3 * ROWS * (i + 1)]
            send[first + i] = part[:ROWS] + part[ROWS : 2 * ROWS] + part[2 * ROWS :]
        return first

    def fill_and_send(group):
        first = fill(group)
        for i in range(GROUP):
            bucket_copy(first + i).start()

    loop(n // GROUP, fill, unrolled)
    pl.semaphore_wait(barrier, n - 1)
    loop(n - 1, lambda i: bucket_copy(i + 1).start(), unrolled)

    for load in loads[5:8]:
        load.wait()
    blocks = active_ref.shape[1]
    row, block = iota((cells, blocks), 0), iota((cells, blocks), 1)
    row_block = row // (4 * size_y) * BY + row % size_y // 4
    by_row = jnp.where(block // BZ == row_block, active_ref[...].astype(F32), 0.0).astype(BF16)
    by_lane = jnp.where(
        iota((LANES, blocks), 1) % BZ == iota((LANES, blocks), 0) // 4, 1.0, 0.0
    ).astype(BF16)
    live = dot_nt(by_row, by_lane)
    tough_ext[pad : pad + cells, :] = live * tough_ref[...]

    low, high = me > 0, me < n - 1
    end = pad + cells

    def upward(array, which, depth):
        return side_copy(
            which, array.at[pl.ds(end - depth, depth)], array.at[pl.ds(pad - depth, depth)], me + 1
        )

    def downward(array, which, depth):
        return side_copy(which, array.at[pl.ds(pad, depth)], array.at[pl.ds(end, depth)], me - 1)

    arrived[0] = send[0]
    total[...] = jnp.zeros_like(total)

    cell = iota((cells, LANES), 0)
    along = iota((LANES, LANES), 0)

    def gather_energy(group):
        lefts, rights = [[], [], []], []
        for i in range(GROUP):
            source = GROUP * group + i
            if not (isinstance(source, int) and source == 0):
                bucket_copy(source).wait_recv()
        for i in range(GROUP):
            source = GROUP * group + i
            rows, code = arrived[source, :8], arrived[source, 9:10].astype(jnp.int32)
            away = cell - code // LANES
            spread = []
            for k in range(2):
                spread.append(
                    jnp.where(
                        away == 0,
                        rows[k : k + 1],
                        jnp.where(
                            away == 1,
                            rows[k + 2 : k + 3],
                            jnp.where(
                                away == size_y,
                                rows[k + 4 : k + 5],
                                jnp.where(away == size_y + 1, rows[k + 6 : k + 7], 0.0),
                            ),
                        ),
                    )
                )
            spread = jnp.concatenate(spread, axis=0)
            mixed[source] = spread
            for held, piece in zip(lefts, pieces(spread * arrived[source, 8:9])):
                held.append(piece)
            hot = jnp.where(along == code % LANES, 1.0, 0.0).astype(BF16)
            zhot[source] = hot
            rights.append(hot)
        left = jnp.concatenate(lefts[0] + lefts[1] + lefts[2], axis=1)
        total[...] += dot_nt(left, jnp.concatenate(rights * 3, axis=1))

    gather_energy(0)
    @pl.when(high)
    def _():
        upward(prior_ext, 0, pad).start()
        upward(tough_ext, 1, inner).start()

    @pl.when(low)
    def _():
        downward(prior_ext, 2, pad).start()
        downward(tough_ext, 3, inner).start()

    loop(n // GROUP - 1, lambda group: gather_energy(group + 1), unrolled)
    energy_ext[pad:end, :] = total[:cells, :] + pltpu.roll(total[cells:, :], 1, 1)

    @pl.when(high)
    def _():
        upward(energy_ext, 4, inner).start()

    @pl.when(low)
    def _():
        downward(energy_ext, 5, inner).start()

    @pl.when(low)
    def _():
        upward(prior_ext, 0, pad).wait_recv()
        upward(tough_ext, 1, inner).wait_recv()
        upward(energy_ext, 4, inner).wait_recv()

    @pl.when(high)
    def _():
        downward(prior_ext, 2, pad).wait_recv()
        downward(tough_ext, 3, inner).wait_recv()
        downward(energy_ext, 5, inner).wait_recv()

    tough = tough_ext[...]
    twice = 2.0 * energy_ext[...]
    alive = tough > 0.0
    under = 1.0 / jnp.where(
        alive, twice + (1.0 / length_scale + 6.0 * length_scale) * tough, 1.0
    )
    couple = length_scale * tough * under
    source = jnp.where(alive, twice * under, 0.0)
    damage = prior_ext[...]
    rows = cells + 2 * pad
    row, lane = iota((rows, LANES), 0) % size_y, iota((rows, LANES), 1)
    blank = jnp.zeros((size_y, LANES), F32)
    for sweep in range(SWEEPS):
        beside = jnp.concatenate([damage[size_y:], blank], axis=0)
        beside = beside + jnp.concatenate([blank, damage[:-size_y]], axis=0)
        beside = beside + jnp.where(row == size_y - 1, 0.0, pltpu.roll(damage, rows - 1, 0))
        beside = beside + jnp.where(row == 0, 0.0, pltpu.roll(damage, 1, 0))
        beside = beside + jnp.where(lane == LANES - 1, 0.0, pltpu.roll(damage, LANES - 1, 1))
        beside = beside + jnp.where(lane == 0, 0.0, pltpu.roll(damage, 1, 1))
        damage = source + couple * beside
    damage = damage[pad:end]
    damage_ref[...] = damage

    both = jnp.concatenate([damage, pltpu.roll(damage, LANES - 1, 1)], axis=0)
    both = jnp.concatenate(pieces(both), axis=1)

    def sample(step):
        first = n - GROUP - GROUP * step
        hot = jnp.concatenate([zhot[first + i] for i in range(GROUP)], axis=1)
        found = dot_nn(both, jnp.concatenate([hot] * 3, axis=0))
        for i in range(GROUP):
            part = found[:, i * LANES : (i + 1) * LANES] * mixed[first + i]
            back_send[first + i] = jnp.sum(part, axis=0, keepdims=True)
        return first

    def sample_and_send(step):
        first = sample(step)
        for i in range(GROUP):
            back_copy(first + i).start()

    loop(n // GROUP - 1, sample_and_send, unrolled)
    sample(n // GROUP - 1)
    for i in range(1, GROUP):
        back_copy(i).start()
    back[0] = back_send[0]
    loop(n - 1, lambda i: back_copy(i + 1).wait_recv(), unrolled)

    returned = jnp.concatenate([back[i] for i in range(n)], axis=0)
    found = dot_nn(jnp.concatenate(pieces(returned), axis=0), place_hot)
    found = found[:n] + found[n : 2 * n] + found[2 * n :]
    particle_damage = jnp.sum(found * owner_hot, axis=0, keepdims=True)
    factor = (1.0 - particle_damage) ** 2 + stiff_floor
    loads[8].wait()
    out_ref[...] = factor * stress_ref[...]

    def finish(i):
        bucket_copy(i + 1).wait_send()
        back_copy(i + 1).wait_send()

    loop(n - 1, finish, unrolled)

    @pl.when(high)
    def _():
        upward(prior_ext, 0, pad).wait_send()
        upward(tough_ext, 1, inner).wait_send()
        upward(energy_ext, 4, inner).wait_send()

    @pl.when(low)
    def _():
        downward(prior_ext, 2, pad).wait_send()
        downward(tough_ext, 3, inner).wait_send()
        downward(energy_ext, 5, inner).wait_send()


def body(
    crack_energy,
    weights,
    elastic_stress,
    owner_rank,
    local_block,
    base_cell,
    prior_damage,
    toughness,
    active_block,
):
    n = lax.axis_size("blk")
    count = crack_energy.shape[0]
    size_x, size_y, size_z = prior_damage.shape
    assert n >= 2 * GROUP and n & (n - 1) == 0
    assert size_z == LANES and 2 * count // n <= LANES and size_x >= SWEEPS
    cells = size_x * size_y
    rows = cells + 2 * SWEEPS * size_y
    vmem = pl.BlockSpec(memory_space=pltpu.VMEM)
    damage, stress = pl.pallas_call(
        functools.partial(kernel, n, size_x, size_y),
        out_shape=(
            pltpu.VMEM((cells, LANES), F32),
            pltpu.VMEM(elastic_stress.shape, F32),
        ),
        in_specs=[pl.BlockSpec(memory_space=pltpu.HBM)] * 9,
        out_specs=(vmem, vmem),
        scratch_shapes=[
            pltpu.VMEM((1, count), F32),
            pltpu.VMEM(weights.shape, F32),
            pltpu.VMEM(elastic_stress.shape, F32),
            pltpu.VMEM((1, count), jnp.int32),
            pltpu.VMEM((1, count), jnp.int32),
            pltpu.VMEM((1, count), jnp.int32),
            pltpu.VMEM((cells, LANES), F32),
            pltpu.VMEM((1, active_block.shape[0]), jnp.int32),
            pltpu.VMEM((n, ROWS, LANES), F32),
            pltpu.VMEM((n, ROWS, LANES), F32),
            pltpu.VMEM((n, 2 * cells, LANES), F32),
            pltpu.VMEM((n, LANES, LANES), BF16),
            pltpu.VMEM((2 * cells, LANES), F32),
            pltpu.VMEM((rows, LANES), F32),
            pltpu.VMEM((rows, LANES), F32),
            pltpu.VMEM((rows, LANES), F32),
            pltpu.VMEM((n, 1, LANES), F32),
            pltpu.VMEM((n, 1, LANES), F32),
            pltpu.SemaphoreType.DMA((n,)),
            pltpu.SemaphoreType.DMA((n,)),
            pltpu.SemaphoreType.DMA((n,)),
            pltpu.SemaphoreType.DMA((n,)),
            pltpu.SemaphoreType.DMA((6,)),
            pltpu.SemaphoreType.DMA((6,)),
            pltpu.SemaphoreType.DMA((9,)),
        ],
        compiler_params=pltpu.CompilerParams(
            collective_id=0,
            has_side_effects=True,
            vmem_limit_bytes=60 * 1024 * 1024,
        ),
    )(
        crack_energy.reshape(1, count),
        weights,
        elastic_stress,
        owner_rank.reshape(1, count),
        local_block.reshape(1, count),
        base_cell.reshape(1, count),
        prior_damage.reshape(cells, LANES),
        toughness.reshape(cells, LANES),
        active_block.reshape(1, active_block.shape[0]),
    )
    return (damage.reshape(prior_damage.shape), stress)


def solution(mesh):
    return jax.shard_map(
        body,
        mesh=mesh,
        in_specs=(
            P(("groups", "blk")),
            P(None, ("groups", "blk")),
            P(None, ("groups", "blk")),
            P(("groups", "blk"), None),
            P(("groups", "blk")),
            P(("groups", "blk")),
            P(("groups", "blk"), None, None),
            P(("groups", "blk"), None, None),
            P(("groups", "blk")),
        ),
        out_specs=(P(("groups", "blk"), None, None), P(None, ("groups", "blk"))),
        check_vma=False,
    )
```

```python
import functools

import jax
import jax.numpy as jnp
from jax import lax
from jax.experimental import pallas as pl
from jax.experimental.pallas import tpu as pltpu
from jax.sharding import PartitionSpec as P

BY = 4
BZ = 32
SWEEPS = 4
LANES = 128
ROWS = 16
USED = 10
GROUP = 4

length_scale = 2.0
stiff_floor = 0.001

F32 = jnp.float32
BF16 = jnp.bfloat16


def iota(shape, axis):
    return lax.broadcasted_iota(jnp.int32, shape, axis)


def pieces(values):
    high = values.astype(BF16)
    rest = values - high.astype(F32)
    middle = rest.astype(BF16)
    low = (rest - middle.astype(F32)).astype(BF16)
    return high, middle, low


def dot_nt(left, right):
    return lax.dot_general(left, right, (((1,), (1,)), ((), ())), preferred_element_type=F32)


def dot_nn(left, right):
    return lax.dot_general(left, right, (((1,), (0,)), ((), ())), preferred_element_type=F32)


def loop(count, step, unrolled):
    if unrolled:
        for i in range(count):
            step(i)
    else:

        @pl.loop(0, count)
        def _(i):
            step(i)


def kernel(
    n,
    size_x,
    size_y,
    energy_in,
    weights_in,
    stress_in,
    owner_in,
    block_in,
    base_in,
    prior_in,
    tough_in,
    active_in,
    damage_ref,
    out_ref,
    energy_ref,
    weights_ref,
    stress_ref,
    owner_ref,
    block_ref,
    base_ref,
    tough_ref,
    active_ref,
    send,
    arrived,
    mixed,
    zhot,
    total,
    energy_ext,
    tough_ext,
    prior_ext,
    back_send,
    back,
    send_sem,
    recv_sem,
    back_send_sem,
    back_recv_sem,
    side_send_sem,
    side_recv_sem,
    load_sem,
):
    me = lax.axis_index("blk")
    cells = size_x * size_y
    count = owner_ref.shape[1]
    pad = SWEEPS * size_y
    loads = [
        pltpu.make_async_copy(source, target, load_sem.at[i])
        for i, (source, target) in enumerate(
            (
                (owner_in, owner_ref),
                (block_in, block_ref),
                (base_in, base_ref),
                (energy_in, energy_ref),
                (weights_in, weights_ref),
                (active_in, active_ref),
                (tough_in, tough_ref),
                (prior_in, prior_ext.at[pl.ds(pad, cells)]),
                (stress_in, stress_ref),
            )
        )
    ]
    for load in loads:
        load.start()
    inner = (SWEEPS - 1) * size_y
    unrolled = n <= 16

    def to(device):
        return {"blk": device}

    def side_copy(which, source, target, device):
        return pltpu.make_async_remote_copy(
            src_ref=source,
            dst_ref=target,
            send_sem=side_send_sem.at[which],
            recv_sem=side_recv_sem.at[which],
            device_id=to(device),
            device_id_type=pl.DeviceIdType.MESH,
        )

    def partner(i):
        device, bit = 0, 1
        while bit < n:
            mine = lax.rem(lax.div(me, jnp.int32(bit)), jnp.int32(2))
            if isinstance(i, int):
                mine = 1 - mine if i // bit % 2 else mine
            else:
                mine = lax.rem(mine + lax.div(i, jnp.int32(bit)), jnp.int32(2))
            device, bit = device + mine * bit, 2 * bit
        return device

    def swap(i, source, target, sends, receives):
        return pltpu.make_async_remote_copy(
            src_ref=source,
            dst_ref=target,
            send_sem=sends.at[i],
            recv_sem=receives.at[i],
            device_id=to(partner(i)),
            device_id_type=pl.DeviceIdType.MESH,
        )

    def bucket_copy(i):
        used = pl.ds(0, USED)
        return swap(i, send.at[i, used], arrived.at[i, used], send_sem, recv_sem)

    def back_copy(i):
        return swap(i, back_send.at[i], back.at[i], back_send_sem, back_recv_sem)

    for array in (energy_ext, tough_ext, prior_ext):
        array[:pad, :] = jnp.zeros((pad, LANES), F32)
        array[pad + cells :, :] = jnp.zeros((pad, LANES), F32)

    barrier = pltpu.get_barrier_semaphore()

    def greet(i):
        pl.semaphore_signal(
            barrier, inc=1, device_id=to(partner(i + 1)), device_id_type=pl.DeviceIdType.MESH
        )

    loop(n - 1, greet, unrolled)

    for load in loads[:5]:
        load.wait()
    owner = jnp.bitwise_xor(owner_ref[...], me)
    owner_hot = jnp.where(iota((n, count), 0) == owner, 1.0, 0.0)
    chunks = count // LANES
    stacked = jnp.concatenate(
        [owner_hot[:, c * LANES : (c + 1) * LANES] for c in range(chunks)], axis=0
    ).astype(BF16)
    ahead = jnp.where(
        (iota((LANES, 2 * LANES), 0) < iota((LANES, 2 * LANES), 1))
        | (iota((LANES, 2 * LANES), 1) >= LANES),
        1.0,
        0.0,
    ).astype(BF16)
    counted = dot_nn(stacked, ahead)
    running = jnp.zeros((n, LANES), F32)
    places = []
    for c in range(chunks):
        part = counted[c * n : (c + 1) * n]
        hot = owner_hot[:, c * LANES : (c + 1) * LANES]
        places.append(jnp.sum(hot * (part[:, :LANES] + running), axis=0, keepdims=True))
        running = running + part[:, LANES:]
    place = jnp.concatenate(places, axis=1).astype(jnp.int32)
    place_hot = jnp.where(iota((LANES, count), 0) == place, 1.0, 0.0).astype(BF16)

    at_block, at_base = block_ref[...], base_ref[...]
    xy = (4 * (at_block // (BY * BZ)) + at_base // 9) * size_y
    xy = xy + 4 * (at_block // BZ % BY) + at_base // 3 % 3
    z = 4 * (at_block % BZ) + at_base % 3
    line = iota((8, count), 0)
    rest = jnp.where(
        line == 0,
        energy_ref[...],
        jnp.where(line == 1, (xy * LANES + z).astype(F32), 0.0),
    )
    payload = pieces(jnp.concatenate([weights_ref[...], rest], axis=0))
    wide_owner = jnp.broadcast_to(owner, (ROWS, count))

    def fill(group):
        first = n - GROUP - GROUP * group
        chosen = []
        for i in range(GROUP):
            mask = jnp.where(wide_owner == first + i, 1.0, 0.0).astype(BF16)
            chosen += [piece * mask for piece in payload]
        bucket = dot_nt(jnp.concatenate(chosen, axis=0), place_hot)
        for i in range(GROUP):
            part = bucket[3 * ROWS * i : 3 * ROWS * (i + 1)]
            send[first + i] = part[:ROWS] + part[ROWS : 2 * ROWS] + part[2 * ROWS :]
        return first

    def fill_and_send(group):
        first = fill(group)
        for i in range(GROUP):
            bucket_copy(first + i).start()

    loop(n // GROUP, fill, unrolled)
    pl.semaphore_wait(barrier, n - 1)
    loop(n - 1, lambda i: bucket_copy(i + 1).start(), unrolled)

    for load in loads[5:8]:
        load.wait()
    blocks = active_ref.shape[1]
    row, block = iota((cells, blocks), 0), iota((cells, blocks), 1)
    row_block = row // (4 * size_y) * BY + row % size_y // 4
    by_row = jnp.where(block // BZ == row_block, active_ref[...].astype(F32), 0.0).astype(BF16)
    by_lane = jnp.where(
        iota((LANES, blocks), 1) % BZ == iota((LANES, blocks), 0) // 4, 1.0, 0.0
    ).astype(BF16)
    live = dot_nt(by_row, by_lane)
    tough_ext[pad : pad + cells, :] = live * tough_ref[...]

    low, high = me > 0, me < n - 1
    end = pad + cells

    def upward(array, which, depth):
        return side_copy(
            which, array.at[pl.ds(end - depth, depth)], array.at[pl.ds(pad - depth, depth)], me + 1
        )

    def downward(array, which, depth):
        return side_copy(which, array.at[pl.ds(pad, depth)], array.at[pl.ds(end, depth)], me - 1)

    arrived[0] = send[0]
    total[...] = jnp.zeros_like(total)

    cell = iota((cells, LANES), 0)
    along = iota((LANES, LANES), 0)

    def gather_energy(group):
        lefts, rights = [[], [], []], []
        for i in range(GROUP):
            source = GROUP * group + i
            if not (isinstance(source, int) and source == 0):
                bucket_copy(source).wait_recv()
        for i in range(GROUP):
            source = GROUP * group + i
            rows, code = arrived[source, :8], arrived[source, 9:10].astype(jnp.int32)
            away = cell - code // LANES
            spread = []
            for k in range(2):
                spread.append(
                    jnp.where(
                        away == 0,
                        rows[k : k + 1],
                        jnp.where(
                            away == 1,
                            rows[k + 2 : k + 3],
                            jnp.where(
                                away == size_y,
                                rows[k + 4 : k + 5],
                                jnp.where(away == size_y + 1, rows[k + 6 : k + 7], 0.0),
                            ),
                        ),
                    )
                )
            spread = jnp.concatenate(spread, axis=0)
            mixed[source] = spread
            for held, piece in zip(lefts, pieces(spread * arrived[source, 8:9])):
                held.append(piece)
            hot = jnp.where(along == code % LANES, 1.0, 0.0).astype(BF16)
            zhot[source] = hot
            rights.append(hot)
        left = jnp.concatenate(lefts[0] + lefts[1] + lefts[2], axis=1)
        total[...] += dot_nt(left, jnp.concatenate(rights * 3, axis=1))

    gather_energy(0)
    @pl.when(high)
    def _():
        upward(prior_ext, 0, pad).start()
        upward(tough_ext, 1, inner).start()

    @pl.when(low)
    def _():
        downward(prior_ext, 2, pad).start()
        downward(tough_ext, 3, inner).start()

    loop(n // GROUP - 1, lambda group: gather_energy(group + 1), unrolled)
    energy_ext[pad:end, :] = total[:cells, :] + pltpu.roll(total[cells:, :], 1, 1)

    @pl.when(high)
    def _():
        upward(energy_ext, 4, inner).start()

    @pl.when(low)
    def _():
        downward(energy_ext, 5, inner).start()

    @pl.when(low)
    def _():
        upward(prior_ext, 0, pad).wait_recv()
        upward(tough_ext, 1, inner).wait_recv()
        upward(energy_ext, 4, inner).wait_recv()

    @pl.when(high)
    def _():
        downward(prior_ext, 2, pad).wait_recv()
        downward(tough_ext, 3, inner).wait_recv()
        downward(energy_ext, 5, inner).wait_recv()

    tough = tough_ext[...]
    twice = 2.0 * energy_ext[...]
    alive = tough > 0.0
    under = 1.0 / jnp.where(
        alive, twice + (1.0 / length_scale + 6.0 * length_scale) * tough, 1.0
    )
    couple = length_scale * tough * under
    source = jnp.where(alive, twice * under, 0.0)
    damage = prior_ext[...]
    rows = cells + 2 * pad
    row, lane = iota((rows, LANES), 0) % size_y, iota((rows, LANES), 1)
    blank = jnp.zeros((size_y, LANES), F32)
    for sweep in range(SWEEPS):
        beside = jnp.concatenate([damage[size_y:], blank], axis=0)
        beside = beside + jnp.concatenate([blank, damage[:-size_y]], axis=0)
        beside = beside + jnp.where(row == size_y - 1, 0.0, pltpu.roll(damage, rows - 1, 0))
        beside = beside + jnp.where(row == 0, 0.0, pltpu.roll(damage, 1, 0))
        beside = beside + jnp.where(lane == LANES - 1, 0.0, pltpu.roll(damage, LANES - 1, 1))
        beside = beside + jnp.where(lane == 0, 0.0, pltpu.roll(damage, 1, 1))
        damage = source + couple * beside
    damage = damage[pad:end]
    damage_ref[...] = damage

    both = jnp.concatenate([damage, pltpu.roll(damage, LANES - 1, 1)], axis=0)
    both = jnp.concatenate(pieces(both), axis=1)

    def sample(step):
        first = n - GROUP - GROUP * step
        hot = jnp.concatenate([zhot[first + i] for i in range(GROUP)], axis=1)
        found = dot_nn(both, jnp.concatenate([hot] * 3, axis=0))
        for i in range(GROUP):
            part = found[:, i * LANES : (i + 1) * LANES] * mixed[first + i]
            back_send[first + i] = jnp.sum(part, axis=0, keepdims=True)
        return first

    def sample_and_send(step):
        first = sample(step)
        for i in range(GROUP):
            back_copy(first + i).start()

    loop(n // GROUP - 1, sample_and_send, unrolled)
    sample(n // GROUP - 1)
    for i in range(1, GROUP):
        back_copy(i).start()
    back[0] = back_send[0]

    def finish(i):
        bucket_copy(i + 1).wait_send()
        back_copy(i + 1).wait_send()

    loop(n - 1, finish, unrolled)

    @pl.when(high)
    def _():
        upward(prior_ext, 0, pad).wait_send()
        upward(tough_ext, 1, inner).wait_send()
        upward(energy_ext, 4, inner).wait_send()

    @pl.when(low)
    def _():
        downward(prior_ext, 2, pad).wait_send()
        downward(tough_ext, 3, inner).wait_send()
        downward(energy_ext, 5, inner).wait_send()

    loop(n - 1, lambda i: back_copy(i + 1).wait_recv(), unrolled)

    returned = jnp.concatenate([back[i] for i in range(n)], axis=0)
    found = dot_nn(jnp.concatenate(pieces(returned), axis=0), place_hot)
    found = found[:n] + found[n : 2 * n] + found[2 * n :]
    particle_damage = jnp.sum(found * owner_hot, axis=0, keepdims=True)
    factor = (1.0 - particle_damage) ** 2 + stiff_floor
    loads[8].wait()
    out_ref[...] = factor * stress_ref[...]


def body(
    crack_energy,
    weights,
    elastic_stress,
    owner_rank,
    local_block,
    base_cell,
    prior_damage,
    toughness,
    active_block,
):
    n = lax.axis_size("blk")
    count = crack_energy.shape[0]
    size_x, size_y, size_z = prior_damage.shape
    assert n >= 2 * GROUP and n & (n - 1) == 0
    assert size_z == LANES and 2 * count // n <= LANES and size_x >= SWEEPS
    cells = size_x * size_y
    rows = cells + 2 * SWEEPS * size_y
    vmem = pl.BlockSpec(memory_space=pltpu.VMEM)
    damage, stress = pl.pallas_call(
        functools.partial(kernel, n, size_x, size_y),
        out_shape=(
            pltpu.VMEM((cells, LANES), F32),
            pltpu.VMEM(elastic_stress.shape, F32),
        ),
        in_specs=[pl.BlockSpec(memory_space=pltpu.HBM)] * 9,
        out_specs=(vmem, vmem),
        scratch_shapes=[
            pltpu.VMEM((1, count), F32),
            pltpu.VMEM(weights.shape, F32),
            pltpu.VMEM(elastic_stress.shape, F32),
            pltpu.VMEM((1, count), jnp.int32),
            pltpu.VMEM((1, count), jnp.int32),
            pltpu.VMEM((1, count), jnp.int32),
            pltpu.VMEM((cells, LANES), F32),
            pltpu.VMEM((1, active_block.shape[0]), jnp.int32),
            pltpu.VMEM((n, ROWS, LANES), F32),
            pltpu.VMEM((n, ROWS, LANES), F32),
            pltpu.VMEM((n, 2 * cells, LANES), F32),
            pltpu.VMEM((n, LANES, LANES), BF16),
            pltpu.VMEM((2 * cells, LANES), F32),
            pltpu.VMEM((rows, LANES), F32),
            pltpu.VMEM((rows, LANES), F32),
            pltpu.VMEM((rows, LANES), F32),
            pltpu.VMEM((n, 1, LANES), F32),
            pltpu.VMEM((n, 1, LANES), F32),
            pltpu.SemaphoreType.DMA((n,)),
            pltpu.SemaphoreType.DMA((n,)),
            pltpu.SemaphoreType.DMA((n,)),
            pltpu.SemaphoreType.DMA((n,)),
            pltpu.SemaphoreType.DMA((6,)),
            pltpu.SemaphoreType.DMA((6,)),
            pltpu.SemaphoreType.DMA((9,)),
        ],
        compiler_params=pltpu.CompilerParams(
            collective_id=0,
            has_side_effects=True,
            vmem_limit_bytes=60 * 1024 * 1024,
        ),
    )(
        crack_energy.reshape(1, count),
        weights,
        elastic_stress,
        owner_rank.reshape(1, count),
        local_block.reshape(1, count),
        base_cell.reshape(1, count),
        prior_damage.reshape(cells, LANES),
        toughness.reshape(cells, LANES),
        active_block.reshape(1, active_block.shape[0]),
    )
    return (damage.reshape(prior_damage.shape), stress)


def solution(mesh):
    return jax.shard_map(
        body,
        mesh=mesh,
        in_specs=(
            P(("groups", "blk")),
            P(None, ("groups", "blk")),
            P(None, ("groups", "blk")),
            P(("groups", "blk"), None),
            P(("groups", "blk")),
            P(("groups", "blk")),
            P(("groups", "blk"), None, None),
            P(("groups", "blk"), None, None),
            P(("groups", "blk")),
        ),
        out_specs=(P(("groups", "blk"), None, None), P(None, ("groups", "blk"))),
        check_vma=False,
    )
```
